32 devices in a mesh: prow: 8 (over y, x, core), pcol: 4 (over z).
Axes of the slice: x: 2, y: 2, z: 4, core: 2. Of those that a mesh axis runs over, the one named last changes fastest.
Arguments:
- matrix: float32 [1024, 8192], P('prow', 'pcol'), as said below
- pivots: int32 [128], replicated, may hold values from 0 to 1023, as said below
Outputs:
- updated: float32 [1024, 8192], P('prow', 'pcol')
The draws below stay inside these ranges and needn't reach their ends.
Inputs may be any that keep to these rules, and one draw needn't show every extreme that they name: pivots[j] is a logical row index from j to 1023; logical row i lies in row block i // 128, held by row process (i // 128) modulo the number of row processes. `matrix`: the strictly lower part of the panel's first 128 rows is small, so that L11 is well conditioned; entries of L21 are at most 1 in magnitude.
All inputs are finite; a program needn't handle non-finite values.
Results may differ from the reference program's by a relative error of at most 0.0003.
Values sent between devices are 32-bit elements; how exact they have to be, the bound alone decides.
A program may use at most 64 MiB of HBM per device.

```python
import jax
import jax.numpy as jnp
from jax import lax

PANEL_BLOCK = 128
ROWS_PER_DEVICE = 128
ACTIVE_ORDER = 1024
NC = 8192


def draw_matrix(key, part):
    key_base = jax.random.fold_in(key, 11)
    key_lower = jax.random.fold_in(key, 12)
    key_diag = jax.random.fold_in(key, 13)
    trailing_draw = jax.random.normal(key_base, (ACTIVE_ORDER, NC), jnp.float32)
    lower_draw = jax.random.uniform(key_lower, (ACTIVE_ORDER, PANEL_BLOCK), jnp.float32, -0.3, 0.3)
    diag_draw = jax.random.uniform(key_diag, (PANEL_BLOCK, PANEL_BLOCK), jnp.float32, -1.0, 1.0) * (2.0 / PANEL_BLOCK)
    row_ids = jnp.arange(PANEL_BLOCK)[:, None]
    col_ids = jnp.arange(PANEL_BLOCK)[None, :]
    top_panel = jnp.where(col_ids < row_ids, diag_draw, trailing_draw[:PANEL_BLOCK, :PANEL_BLOCK])
    panel_cols = jnp.concatenate([top_panel, lower_draw[PANEL_BLOCK:]], axis=0)
    return jnp.concatenate([panel_cols, trailing_draw[:, PANEL_BLOCK:]], axis=1)


def draw_pivots(key, part):
    raw_draw = jax.random.randint(jax.random.fold_in(key, 21), (PANEL_BLOCK,), 0, ACTIVE_ORDER, dtype=jnp.int32)
    first_row = jnp.arange(PANEL_BLOCK, dtype=jnp.int32)
    return (first_row + raw_draw % (ACTIVE_ORDER - first_row)).astype(jnp.int32)


def setup_inputs(seed: int = 0) -> dict:
    arg_keys = jax.random.split(jax.random.key(seed), 3)
    matrix = draw_matrix(jax.random.fold_in(arg_keys[2], 71), 0)
    pivots = draw_pivots(jax.random.fold_in(arg_keys[2], 71), 0)
    return dict(matrix=matrix, pivots=pivots)


def reference(matrix, pivots):

    def swap_pair(j, order):
        pivot_row = pivots[j]
        first_val = order[j]
        second_val = order[pivot_row]
        order = order.at[j].set(second_val)
        return order.at[pivot_row].set(first_val)
    order = lax.fori_loop(0, PANEL_BLOCK, swap_pair, jnp.arange(ACTIVE_ORDER, dtype=jnp.int32))
    process_count = ACTIVE_ORDER // ROWS_PER_DEVICE
    stored_positions = jnp.arange(ACTIVE_ORDER, dtype=jnp.int32)
    local_positions = stored_positions % ROWS_PER_DEVICE
    logical_position = ((local_positions // PANEL_BLOCK * process_count + stored_positions // ROWS_PER_DEVICE) * PANEL_BLOCK + local_positions % PANEL_BLOCK).astype(jnp.int32)
    source_logical_row = order[logical_position]
    block_numbers = source_logical_row // PANEL_BLOCK
    source_stored_row = (block_numbers % process_count * ROWS_PER_DEVICE + block_numbers // process_count * PANEL_BLOCK + source_logical_row % PANEL_BLOCK).astype(jnp.int32)
    swapped = jnp.take(matrix[:, PANEL_BLOCK:], source_stored_row, axis=0)
    lower_unit = jnp.tril(matrix[:PANEL_BLOCK, :PANEL_BLOCK], -1) + jnp.eye(PANEL_BLOCK, dtype=jnp.float32)
    upper_rows = jax.scipy.linalg.solve_triangular(lower_unit, swapped[:PANEL_BLOCK], lower=True, unit_diagonal=True)
    lower_rest = swapped[PANEL_BLOCK:] - jnp.dot(matrix[PANEL_BLOCK:, :PANEL_BLOCK].astype(jnp.float32), upper_rows.astype(jnp.float32), precision=lax.Precision.HIGHEST, preferred_element_type=jnp.float32)
    trailing = jnp.concatenate([upper_rows, lower_rest], axis=0)
    return jnp.concatenate([matrix[:, :PANEL_BLOCK], trailing], axis=1)
```

```python
import functools

import jax
import jax.numpy as jnp
from jax import lax
from jax.experimental import pallas as pl
from jax.experimental.pallas import tpu as pltpu
from jax.sharding import PartitionSpec as P

MESH = pl.DeviceIdType.MESH
TOP_PIECES = 4
TILE = 256


def mm(a, b):
    return jnp.dot(a, b, preferred_element_type=jnp.float32)


def split(x):
    high = x.astype(jnp.bfloat16)
    low = (x - high.astype(jnp.float32)).astype(jnp.bfloat16)
    return high, low


def mm3(a, b):
    ah, al = split(a)
    bh, bl = split(b)
    return mm(ah, bh) + (mm(ah, bl) + mm(al, bh))


def kernel(
    procs, cols_procs, grid_x, a_ref, piv_ref, out_ref,
    abuf, top, hi, lo, cbuf, rbuf, gbuf, base, obuf, pan, l11, kbuf, proj,
    ex_sem, pz_send, pz_recv, pp_sem, l_send, l_recv, k_sem,
    rs_send, rs_recv, ag_send, ag_recv, t_send, t_recv, o_sem,
):
    B, cols = a_ref.shape
    half = cols // 2
    chips = procs // 2
    rc = B // chips
    rp = B // TOP_PIECES
    me = lax.axis_index("prow")
    z = lax.axis_index("pcol")
    chip = me // 2
    core = me % 2
    peer = chip * 2 + 1 - core

    def remote(src, dst, send, recv, device):
        return pltpu.make_async_remote_copy(
            src_ref=src, dst_ref=dst, send_sem=send, recv_sem=recv,
            device_id=device, device_id_type=MESH,
        )

    def snake(k):
        y, x = k // grid_x, k % grid_x
        odd = y % 2
        return y * grid_x + x + odd * (grid_x - 1 - 2 * x)

    def other(d):
        return (chip + d) % chips

    def rows_of(k):
        return pl.ds(pl.multiple_of(k * rc, rc), rc)

    barrier = pltpu.get_barrier_semaphore()
    greeted = [(peer, z)]
    greeted += [(other(d) * 2 + core, z) for d in range(1, chips)]
    greeted += [(me, (z + d) % cols_procs) for d in range(1, cols_procs)]
    for device in greeted:
        pl.semaphore_signal(barrier, inc=1, device_id=device, device_id_type=MESH)
    pl.semaphore_wait(barrier, len(greeted))

    mine = pl.ds(pl.multiple_of(core * half, half), half)
    theirs = pl.ds(pl.multiple_of((1 - core) * half, half), half)
    exchange = remote(
        a_ref.at[:, theirs], abuf.at[core], ex_sem.at[0], ex_sem.at[1], (peer, z)
    )
    exchange.start()

    panel_z = [
        remote(
            a_ref.at[:, pl.ds(0, B)], pan.at[core],
            pz_send.at[d - 1], pz_recv.at[0], (me, (z + d) % cols_procs),
        )
        for d in range(1, cols_procs)
    ]

    @pl.when(z == 0)
    def _():
        for copy in panel_z:
            copy.start()
        pan[core] = a_ref[:, :B]

    row = lax.broadcasted_iota(jnp.int32, (B, B), 0)
    col = lax.broadcasted_iota(jnp.int32, (B, B), 1)
    eye = row == col
    piv = piv_ref[...]
    pr = jnp.broadcast_to(piv, (B, B))
    pc = jnp.sum(jnp.where(eye, pr, 0), axis=1, keepdims=True)
    colf = col.astype(jnp.float32)
    before = col < row

    def last(mask, lanes):
        return jnp.max(jnp.where(mask, lanes, -1.0), axis=1, keepdims=True)

    prev = last((pc == pr) & before, colf)
    parent = last((pr == row) & before, colf)
    root_self = parent < 0
    hot = jnp.where(
        root_self, jnp.where(eye, 1.0, 0.0), jnp.where(colf == parent, 1.0, 0.0)
    ).astype(jnp.bfloat16)
    steps = 1
    while steps < B:
        hot = mm(hot, hot).astype(jnp.bfloat16)
        steps *= 2
    from_prev = mm(jnp.where(colf == prev, 1.0, 0.0).astype(jnp.bfloat16), hot)

    first = chip * (2 * B)
    col2 = lax.broadcasted_iota(jnp.int32, (B, 2 * B), 1)
    on_first = (chip == 0).astype(jnp.float32)
    direct = jnp.where((prev < 0) & (pc == col2 + first), 1.0, 0.0)
    pick = jnp.concatenate(
        [direct[:, :B] + on_first * from_prev, direct[:, B:]], axis=1
    ).astype(jnp.bfloat16)

    row2 = lax.broadcasted_iota(jnp.int32, (2 * B, B), 0)
    col3 = lax.broadcasted_iota(jnp.int32, (2 * B, B), 1).astype(jnp.float32)
    logical = row2 + first
    filled = last(jnp.broadcast_to(piv, (2 * B, B)) == logical, col3)
    is_rest = logical[:, :1] >= B
    fill = jnp.where((col3 == filled) & (logical >= B), 1.0, 0.0)
    fill = mm(fill.astype(jnp.bfloat16), hot).astype(jnp.bfloat16)
    keep = jnp.where(is_rest & (filled < 0), 1.0, 0.0)

    own_rows = pl.ds(pl.multiple_of(core * B, B), B)
    peer_rows = pl.ds(pl.multiple_of((1 - core) * B, B), B)
    h, l = split(a_ref[:, mine])
    hi[own_rows, :] = h
    lo[own_rows, :] = l

    step = 1 - 2 * core
    place = snake(chip)
    rank = (place * step + chips) % chips
    onward = snake((place + step + chips) % chips) * 2 + core
    top_copies = [
        remote(
            top.at[pl.ds(i * rp, rp)], top.at[pl.ds(i * rp, rp)],
            t_send.at[i], t_recv.at[i], (onward, z),
        )
        for i in range(TOP_PIECES)
    ]

    @pl.when(me == 0)
    def _():
        top[...] = a_ref[:, :half]

    exchange.wait_recv()

    @pl.when(me == 1)
    def _():
        top[...] = abuf[0]

    @pl.when(chip == 0)
    def _():
        for copy in top_copies:
            copy.start()

    h, l = split(abuf[1 - core])
    hi[peer_rows, :] = h
    lo[peer_rows, :] = l

    to_zero = remote(pan.at[core], pan.at[core], pp_sem.at[0], pp_sem.at[1], (peer, z))
    l_copies = [
        remote(pan.at[0], l11, l_send.at[d - 1], l_recv.at[0], (other(d) * 2 + core, z))
        for d in range(1, chips)
    ]

    @pl.when(z != 0)
    def _():
        panel_z[0].wait_recv()

    @pl.when(core == 1)
    def _():
        to_zero.start()

    @pl.when(me == 0)
    def _():
        for copy in l_copies:
            copy.start()
        l11[...] = pan[0]

    for t in range(0, half, TILE):
        s = pl.ds(t, TILE)
        cbuf[:, s] = mm(pick, hi[:, s]) + mm(pick, lo[:, s])
    rs = [
        remote(
            cbuf.at[rows_of(other(d))], rbuf.at[d - 1],
            rs_send.at[d - 1], rs_recv.at[d - 1], (other(d) * 2 + core, z),
        )
        for d in range(1, chips)
    ]
    for copy in rs:
        copy.start()

    def forward(i):
        @pl.when(rank > 0)
        def _():
            top_copies[i].wait_recv()

        @pl.when((rank > 0) & (rank < chips - 1))
        def _():
            top_copies[i].start()

    proj[:, :] = fill

    forward(0)

    @pl.when((core == 0) & (chip != 0))
    def _():
        l_copies[0].wait_recv()

    @pl.when(core == 0)
    def _():
        to_zero.wait_recv()

    levels = []
    size = 2
    while size < B:
        levels.append(size)
        size *= 2

    def off_diagonal(size):
        same = (row & (-2 * size)) == (col & (-2 * size))
        return jnp.where(
            same & ((row & size) != 0) & ((col & size) == 0), l11[...], 0.0
        )

    def advance(sizes):
        @pl.when(core == 0)
        def _():
            x = kbuf[:B, :]
            for size in sizes:
                x = x - mm3(x, mm3(off_diagonal(size), x))
            kbuf[:B, :] = x

    @pl.when(core == 0)
    def _():
        kbuf[:B, :] = jnp.where(eye, 1.0, 0.0) - off_diagonal(1)

    at = 0
    for i in range(1, TOP_PIECES):
        upto = len(levels) * i // (TOP_PIECES - 1)
        advance(levels[at:upto])
        at = upto
        forward(i)

    k_copy = remote(kbuf, kbuf, k_sem.at[0], k_sem.at[1], (peer, z))

    @pl.when(core == 0)
    def _():
        inverse = kbuf[:B, :]
        lead = on_first * jnp.where(eye, 1.0, 0.0) - (1.0 - on_first) * pan[0]
        low_part = mm3(pan[1], inverse)
        kbuf[:B, :] = mm3(lead, inverse)
        kbuf[B:, :] = -low_part
        k_copy.start()

    for copy in rs:
        copy.wait_recv()
    total = cbuf[rows_of(chip), :]
    for d in range(1, chips):
        total = total + rbuf[d - 1]
    gbuf[rows_of(chip), :] = total
    ag = [
        remote(
            gbuf.at[rows_of(chip)], gbuf.at[rows_of(chip)],
            ag_send.at[d - 1], ag_recv.at[d - 1], (other(d) * 2 + core, z),
        )
        for d in range(1, chips)
    ]
    for copy in ag:
        copy.start()

    own_keep = jnp.where(core == 0, keep[:B], keep[B:])
    peer_keep = jnp.where(core == 0, keep[B:], keep[:B])
    base[own_rows, :] = own_keep * a_ref[:, mine]
    base[peer_rows, :] = peer_keep * abuf[1 - core]
    for t in range(0, half, TILE):
        s = pl.ds(t, TILE)
        th, tl = split(top[:, s])
        base[:, s] = base[:, s] + (mm(proj[...], th) + mm(proj[...], tl))

    @pl.when(core == 1)
    def _():
        k_copy.wait_recv()

    kh_peer, kl_peer = split(kbuf[peer_rows, :])
    kh_own, kl_own = split(kbuf[own_rows, :])
    for d in range(1, chips):
        came = (chip - d + chips) % chips
        remote(
            gbuf.at[rows_of(came)], gbuf.at[rows_of(came)],
            ag_send.at[d - 1], ag_recv.at[d - 1], (other(d) * 2 + core, z),
        ).wait_recv()

    out_peer = remote(obuf.at[0], out_ref.at[:, mine], o_sem.at[0], o_sem.at[1], (peer, z))
    out_own = pltpu.make_async_copy(obuf.at[1], out_ref.at[:, mine], o_sem.at[2])
    for t in range(0, half, TILE):
        s = pl.ds(t, TILE)
        gh, gl = split(gbuf[:, s])
        obuf[0, :, s] = base[peer_rows, s] + (
            mm(kh_peer, gh) + (mm(kh_peer, gl) + mm(kl_peer, gh))
        )
    out_peer.start()
    for t in range(0, half, TILE):
        s = pl.ds(t, TILE)
        gh, gl = split(gbuf[:, s])
        obuf[1, :, s] = base[own_rows, s] + (
            mm(kh_own, gh) + (mm(kh_own, gl) + mm(kl_own, gh))
        )
    out_own.start()

    exchange.wait_send()

    @pl.when(z == 0)
    def _():
        for copy in panel_z:
            copy.wait_send()

    @pl.when(core == 1)
    def _():
        to_zero.wait_send()

    @pl.when(core == 0)
    def _():
        k_copy.wait_send()

    @pl.when(me == 0)
    def _():
        for copy in l_copies:
            copy.wait_send()

    @pl.when(rank < chips - 1)
    def _():
        for copy in top_copies:
            copy.wait_send()

    for copy in rs + ag:
        copy.wait_send()
    out_own.wait()
    remote(
        obuf.at[0], out_ref.at[:, theirs], o_sem.at[0], o_sem.at[1], (peer, z)
    ).wait_recv()
    out_peer.wait_send()


def local(procs, cols_procs, matrix, pivots):
    B, cols = matrix.shape
    half = cols // 2
    chips = procs // 2
    grid_x = 1
    while (grid_x * 2) * (grid_x * 2) <= chips:
        grid_x *= 2
    f32, bf16 = jnp.float32, jnp.bfloat16
    dma = pltpu.SemaphoreType.DMA
    stepped = pl.pallas_call(
        functools.partial(kernel, procs, cols_procs, grid_x),
        out_shape=jax.ShapeDtypeStruct((B, cols), f32),
        in_specs=[pl.BlockSpec(memory_space=pltpu.VMEM)] * 2,
        out_specs=pl.BlockSpec(memory_space=pl.ANY),
        scratch_shapes=[
            pltpu.VMEM((2, B, half), f32),
            pltpu.VMEM((B, half), f32),
            pltpu.VMEM((2 * B, half), bf16),
            pltpu.VMEM((2 * B, half), bf16),
            pltpu.VMEM((B, half), f32),
            pltpu.VMEM((chips - 1, B // chips, half), f32),
            pltpu.VMEM((B, half), f32),
            pltpu.VMEM((2 * B, half), f32),
            pltpu.VMEM((2, B, half), f32),
            pltpu.VMEM((2, B, B), f32),
            pltpu.VMEM((B, B), f32),
            pltpu.VMEM((2 * B, B), f32),
            pltpu.VMEM((2 * B, B), bf16),
            dma((2,)),
            dma((cols_procs - 1,)),
            dma((1,)),
            dma((2,)),
            dma((chips - 1,)),
            dma((1,)),
            dma((2,)),
            dma((chips - 1,)),
            dma((chips - 1,)),
            dma((chips - 1,)),
            dma((chips - 1,)),
            dma((TOP_PIECES,)),
            dma((TOP_PIECES,)),
            dma((3,)),
        ],
        compiler_params=pltpu.CompilerParams(
            collective_id=0, has_side_effects=True, vmem_limit_bytes=32 * 1024 * 1024
        ),
    )(matrix, pivots.reshape(1, -1))
    col_ids = jnp.arange(cols, dtype=jnp.int32)
    keep_panel = (lax.axis_index("pcol") == 0) & (col_ids < pivots.shape[0])
    return jnp.where(keep_panel[None, :], matrix, stepped)


def solution(mesh):
    body = functools.partial(local, mesh.shape["prow"], mesh.shape["pcol"])
    return jax.shard_map(
        body, mesh=mesh, in_specs=(P("prow", "pcol"), P()),
        out_specs=P("prow", "pcol"), check_vma=False,
    )
```

```python
import functools

import jax
import jax.numpy as jnp
from jax import lax
from jax.experimental import pallas as pl
from jax.experimental.pallas import tpu as pltpu
from jax.sharding import PartitionSpec as P

MESH = pl.DeviceIdType.MESH
TOP_PIECES = 4
EARLY = 2
TILE = 256


def mm(a, b):
    return jnp.dot(a, b, preferred_element_type=jnp.float32)


def split(x):
    high = x.astype(jnp.bfloat16)
    low = (x - high.astype(jnp.float32)).astype(jnp.bfloat16)
    return high, low


def mm3(a, b):
    ah, al = split(a)
    bh, bl = split(b)
    return mm(ah, bh) + (mm(ah, bl) + mm(al, bh))


def kernel(
    procs, cols_procs, grid_x, a_ref, piv_ref, out_ref,
    abuf, top, hi, lo, cbuf, rbuf, hbuf, qbuf, gbuf, base, obuf, pan, l11, kbuf, proj,
    in_sem, ex_sem, pz_send, pz_recv, pp_sem, l_send, l_recv, k_sem,
    rs_send, rs_recv, hs_send, hs_recv, ag_send, ag_recv, fw_send, fw_recv,
    t_send, t_recv, p_send, p_recv, o_sem,
):
    B, cols = a_ref.shape
    half = cols // 2
    chips = procs // 2
    rc = B // chips
    rp = B // TOP_PIECES
    me = lax.axis_index("prow")
    z = lax.axis_index("pcol")
    chip = me // 2
    core = me % 2
    peer = chip * 2 + 1 - core

    def remote(src, dst, send, recv, device):
        return pltpu.make_async_remote_copy(
            src_ref=src, dst_ref=dst, send_sem=send, recv_sem=recv,
            device_id=device, device_id_type=MESH,
        )

    def snake(k):
        across, down = k % grid_x, k // grid_x
        return down * grid_x + across + down % 2 * (grid_x - 1 - 2 * across)

    n = grid_x
    y, x = chip // n, chip % n
    u = x + core * (y - x)
    v = y + core * (x - y)

    def at_uv(uu, vv):
        return (uu + core * (vv - uu)) + n * (vv + core * (uu - vv))

    def along_u(d):
        return at_uv((u + d) % n, v) * 2 + core, z

    def along_v(d):
        return at_uv(u, (v + d) % n) * 2 + core, z

    def rows_of(k, count=1):
        return pl.ds(pl.multiple_of(k * rc, rc), count * rc)

    mine = pl.ds(pl.multiple_of(core * half, half), half)
    theirs = pl.ds(pl.multiple_of((1 - core) * half, half), half)
    load = pltpu.make_async_copy(a_ref.at[:, mine], abuf.at[core], in_sem.at[0])
    load.start()
    load_panel = pltpu.make_async_copy(
        a_ref.at[:, pl.ds(0, B)], pan.at[core], in_sem.at[1]
    )

    @pl.when(z == 0)
    def _():
        load_panel.start()

    step = 1 - 2 * core
    place = snake(chip)
    rank = (place * step + chips) % chips
    onward = snake((place + step + chips) % chips) * 2 + core
    behind = snake((place - step + chips) % chips) * 2 + core

    barrier = pltpu.get_barrier_semaphore()
    greeted = [(peer, z)]
    greeted += [along_u(d) for d in range(1, n)]
    greeted += [along_v(d) for d in range(1, n)]
    greeted += [(onward, z), (behind, z)] if n > 2 else []
    greeted += [(me, (z + d) % cols_procs) for d in range(1, cols_procs)]
    for device in greeted:
        pl.semaphore_signal(barrier, inc=1, device_id=device, device_id_type=MESH)

    row = lax.broadcasted_iota(jnp.int32, (B, B), 0)
    col = lax.broadcasted_iota(jnp.int32, (B, B), 1)
    eye = row == col
    piv = piv_ref[...]
    pr = jnp.broadcast_to(piv, (B, B))
    pc = jnp.sum(jnp.where(eye, pr, 0), axis=1, keepdims=True)
    colf = col.astype(jnp.float32)
    before = col < row

    def last(mask, lanes):
        return jnp.max(jnp.where(mask, lanes, -1.0), axis=1, keepdims=True)

    prev = last((pc == pr) & before, colf)
    parent = last((pr == row) & before, colf)
    root_self = parent < 0
    hot = jnp.where(
        root_self, jnp.where(eye, 1.0, 0.0), jnp.where(colf == parent, 1.0, 0.0)
    ).astype(jnp.bfloat16)
    pl.semaphore_wait(barrier, len(greeted))

    exchange = remote(
        a_ref.at[:, theirs], abuf.at[core], ex_sem.at[0], ex_sem.at[1], (peer, z)
    )
    exchange.start()

    panel_z = [
        remote(
            a_ref.at[:, pl.ds(0, B)], pan.at[core],
            pz_send.at[d - 1], pz_recv.at[0], (me, (z + d) % cols_procs),
        )
        for d in range(1, cols_procs)
    ]

    @pl.when(z == 0)
    def _():
        for copy in panel_z:
            copy.start()

    top_copies = [
        remote(
            top.at[pl.ds(i * rp, rp)], top.at[pl.ds(i * rp, rp)],
            t_send.at[i], t_recv.at[i], (onward, z),
        )
        for i in range(TOP_PIECES)
    ]

    load.wait()

    @pl.when(me == 0)
    def _():
        top[...] = abuf[0]
        for copy in top_copies[:EARLY]:
            copy.start()

    steps = 1
    while steps < B:
        hot = mm(hot, hot).astype(jnp.bfloat16)
        steps *= 2
    from_prev = mm(jnp.where(colf == prev, 1.0, 0.0).astype(jnp.bfloat16), hot)

    first = chip * (2 * B)
    col2 = lax.broadcasted_iota(jnp.int32, (B, 2 * B), 1)
    on_first = (chip == 0).astype(jnp.float32)
    direct = jnp.where((prev < 0) & (pc == col2 + first), 1.0, 0.0)
    pick = jnp.concatenate(
        [direct[:, :B] + on_first * from_prev, direct[:, B:]], axis=1
    ).astype(jnp.bfloat16)

    row2 = lax.broadcasted_iota(jnp.int32, (2 * B, B), 0)
    col3 = lax.broadcasted_iota(jnp.int32, (2 * B, B), 1).astype(jnp.float32)
    logical = row2 + first
    filled = last(jnp.broadcast_to(piv, (2 * B, B)) == logical, col3)
    is_rest = logical[:, :1] >= B
    fill = jnp.where((col3 == filled) & (logical >= B), 1.0, 0.0)
    fill = mm(fill.astype(jnp.bfloat16), hot).astype(jnp.bfloat16)
    keep = jnp.where(is_rest & (filled < 0), 1.0, 0.0)

    own_rows = pl.ds(pl.multiple_of(core * B, B), B)
    peer_rows = pl.ds(pl.multiple_of((1 - core) * B, B), B)
    h, l = split(abuf[core])
    hi[own_rows, :] = h
    lo[own_rows, :] = l

    exchange.wait_recv()

    @pl.when(me == 1)
    def _():
        top[...] = abuf[0]
        for copy in top_copies[:EARLY]:
            copy.start()

    h, l = split(abuf[1 - core])
    hi[peer_rows, :] = h
    lo[peer_rows, :] = l

    to_zero = remote(pan.at[core], pan.at[core], pp_sem.at[0], pp_sem.at[1], (peer, z))
    l_first = [
        remote(pan.at[0], l11, l_send.at[d - 1], l_recv.at[0], along_u(d))
        for d in range(1, n)
    ]
    l_then = [
        remote(l11, l11, l_send.at[n - 2 + d], l_recv.at[0], along_v(d))
        for d in range(1, n)
    ]

    @pl.when(z != 0)
    def _():
        panel_z[0].wait_recv()

    @pl.when(z == 0)
    def _():
        load_panel.wait()

    @pl.when(core == 1)
    def _():
        to_zero.start()

    @pl.when(me == 0)
    def _():
        for copy in l_first:
            copy.start()
        l11[...] = pan[0]
        for copy in l_then:
            copy.start()

    for t in range(0, half, TILE):
        s = pl.ds(t, TILE)
        cbuf[:, s] = mm(pick, hi[:, s]) + mm(pick, lo[:, s])
    rs = [
        remote(
            cbuf.at[rows_of((u + d) % n * n, n)], rbuf.at[d - 1],
            rs_send.at[d - 1], rs_recv.at[d - 1], along_u(d),
        )
        for d in range(1, n)
    ]
    for copy in rs:
        copy.start()

    @pl.when(rank == 0)
    def _():
        for copy in top_copies[EARLY:]:
            copy.start()

    def forward(i):
        @pl.when((rank > 0) & (rank < chips - 1))
        def _():
            top_copies[i].wait_recv()
            top_copies[i].start()

    proj[:, :] = fill

    forward(0)

    @pl.when((core == 0) & (chip != 0))
    def _():
        l_first[0].wait_recv()

    @pl.when((core == 0) & (chip != 0) & (y == 0))
    def _():
        for copy in l_then:
            copy.start()

    @pl.when(core == 0)
    def _():
        to_zero.wait_recv()

    levels = []
    size = 2
    while size < B:
        levels.append(size)
        size *= 2

    def off_diagonal(size):
        same = (row & (-2 * size)) == (col & (-2 * size))
        return jnp.where(
            same & ((row & size) != 0) & ((col & size) == 0), l11[...], 0.0
        )

    def advance(sizes):
        @pl.when(core == 0)
        def _():
            x = kbuf[:B, :]
            for size in sizes:
                x = x - mm3(x, mm3(off_diagonal(size), x))
            kbuf[:B, :] = x

    @pl.when(core == 0)
    def _():
        kbuf[:B, :] = jnp.where(eye, 1.0, 0.0) - off_diagonal(1)

    cut = (len(levels) + 1) // 3
    advance(levels[:cut])
    for copy in rs:
        copy.wait_recv()
    total = cbuf[rows_of(u * n, n), :]
    for d in range(1, n):
        total = total + rbuf[d - 1]
    hbuf[...] = total
    hs = [
        remote(
            hbuf.at[rows_of((v + d) % n)], qbuf.at[d - 1],
            hs_send.at[d - 1], hs_recv.at[d - 1], along_v(d),
        )
        for d in range(1, n)
    ]
    for copy in hs:
        copy.start()
    forward(1)
    advance(levels[cut : 2 * cut])
    for copy in hs:
        copy.wait_recv()
    total = hbuf[rows_of(v), :]
    for d in range(1, n):
        total = total + qbuf[d - 1]
    own_chunk = rows_of(u * n + v)
    gbuf[own_chunk, :] = total

    ag = [
        remote(
            gbuf.at[own_chunk], gbuf.at[own_chunk],
            ag_send.at[d - 1], ag_recv.at[d - 1], along_v(d),
        )
        for d in range(1, n)
    ]
    fw = []
    for e in range(n):
        chunk = rows_of(u * n + (v - e + n) % n)
        fw.append([
            remote(
                gbuf.at[chunk], gbuf.at[chunk],
                fw_send.at[e * (n - 1) + d - 1], fw_recv.at[e * (n - 1) + d - 1],
                along_u(d),
            )
            for d in range(1, n)
        ])
    for copy in ag + fw[0]:
        copy.start()
    for i in range(2, TOP_PIECES):
        forward(i)
    advance(levels[2 * cut :])
    for e in range(1, n):
        chunk = rows_of(u * n + (v - e + n) % n)
        remote(
            gbuf.at[chunk], gbuf.at[chunk],
            ag_send.at[e - 1], ag_recv.at[e - 1], along_v(e),
        ).wait_recv()
        for copy in fw[e]:
            copy.start()

    k_copy = remote(kbuf, kbuf, k_sem.at[0], k_sem.at[1], (peer, z))

    @pl.when(core == 0)
    def _():
        inverse = kbuf[:B, :]
        lead = on_first * jnp.where(eye, 1.0, 0.0) - (1.0 - on_first) * pan[0]
        low_part = mm3(pan[1], inverse)
        kbuf[:B, :] = mm3(lead, inverse)
        kbuf[B:, :] = -low_part
        k_copy.start()

    @pl.when(rank == chips - 1)
    def _():
        for copy in top_copies:
            copy.wait_recv()

    base[:B, :] = keep[:B] * abuf[0]
    base[B:, :] = keep[B:] * abuf[1]
    for t in range(0, half, TILE):
        s = pl.ds(t, TILE)
        th, tl = split(top[:, s])
        base[:, s] = base[:, s] + (mm(proj[...], th) + mm(proj[...], tl))

    @pl.when(core == 1)
    def _():
        k_copy.wait_recv()

    kh_peer, kl_peer = split(kbuf[peer_rows, :])
    kh_own, kl_own = split(kbuf[own_rows, :])
    for e in range(n):
        for d in range(1, n):
            chunk = rows_of((u - d + n) % n * n + (v - e + n) % n)
            remote(
                gbuf.at[chunk], gbuf.at[chunk],
                fw_send.at[e * (n - 1) + d - 1], fw_recv.at[e * (n - 1) + d - 1],
                along_u(d),
            ).wait_recv()

    def tile_of(side, t):
        return pl.ds(pl.multiple_of(side * half + t, TILE), TILE)

    tiles = range(0, half, TILE)
    out_peer = [
        remote(
            obuf.at[0, :, pl.ds(t, TILE)], out_ref.at[:, tile_of(core, t)],
            p_send.at[t // TILE], p_recv.at[t // TILE], (peer, z),
        )
        for t in tiles
    ]
    out_own = pltpu.make_async_copy(obuf.at[1], out_ref.at[:, mine], o_sem.at[0])
    for t in tiles:
        s = pl.ds(t, TILE)
        gh, gl = split(gbuf[:, s])
        obuf[0, :, s] = base[peer_rows, s] + (
            mm(kh_peer, gh) + (mm(kh_peer, gl) + mm(kl_peer, gh))
        )
        out_peer[t // TILE].start()
    for t in tiles:
        s = pl.ds(t, TILE)
        gh, gl = split(gbuf[:, s])
        obuf[1, :, s] = base[own_rows, s] + (
            mm(kh_own, gh) + (mm(kh_own, gl) + mm(kl_own, gh))
        )
    out_own.start()

    exchange.wait_send()

    @pl.when(z == 0)
    def _():
        for copy in panel_z:
            copy.wait_send()

    @pl.when(core == 1)
    def _():
        to_zero.wait_send()

    @pl.when(core == 0)
    def _():
        k_copy.wait_send()

    @pl.when(me == 0)
    def _():
        for copy in l_first:
            copy.wait_send()

    @pl.when((core == 0) & (y == 0))
    def _():
        for copy in l_then:
            copy.wait_send()

    @pl.when(rank < chips - 1)
    def _():
        for copy in top_copies:
            copy.wait_send()

    for copy in rs + hs + ag + [c for part in fw for c in part]:
        copy.wait_send()
    out_own.wait()
    for t in tiles:
        remote(
            obuf.at[0, :, pl.ds(t, TILE)], out_ref.at[:, tile_of(1 - core, t)],
            p_send.at[t // TILE], p_recv.at[t // TILE], (peer, z),
        ).wait_recv()
    for copy in out_peer:
        copy.wait_send()


def local(procs, cols_procs, matrix, pivots):
    B, cols = matrix.shape
    half = cols // 2
    chips = procs // 2
    n = 1
    while n * n < chips:
        n += 1
    f32, bf16 = jnp.float32, jnp.bfloat16
    dma = pltpu.SemaphoreType.DMA
    stepped = pl.pallas_call(
        functools.partial(kernel, procs, cols_procs, n),
        out_shape=jax.ShapeDtypeStruct((B, cols), f32),
        in_specs=[
            pl.BlockSpec(memory_space=pltpu.HBM),
            pl.BlockSpec(memory_space=pltpu.VMEM),
        ],
        out_specs=pl.BlockSpec(memory_space=pl.ANY),
        scratch_shapes=[
            pltpu.VMEM((2, B, half), f32),
            pltpu.VMEM((B, half), f32),
            pltpu.VMEM((2 * B, half), bf16),
            pltpu.VMEM((2 * B, half), bf16),
            pltpu.VMEM((B, half), f32),
            pltpu.VMEM((n - 1, B // n, half), f32),
            pltpu.VMEM((B // n, half), f32),
            pltpu.VMEM((n - 1, B // chips, half), f32),
            pltpu.VMEM((B, half), f32),
            pltpu.VMEM((2 * B, half), f32),
            pltpu.VMEM((2, B, half), f32),
            pltpu.VMEM((2, B, B), f32),
            pltpu.VMEM((B, B), f32),
            pltpu.VMEM((2 * B, B), f32),
            pltpu.VMEM((2 * B, B), bf16),
            dma((2,)),
            dma((2,)),
            dma((cols_procs - 1,)),
            dma((1,)),
            dma((2,)),
            dma((2 * (n - 1),)),
            dma((1,)),
            dma((2,)),
            dma((n - 1,)),
            dma((n - 1,)),
            dma((n - 1,)),
            dma((n - 1,)),
            dma((n - 1,)),
            dma((n - 1,)),
            dma((n * (n - 1),)),
            dma((n * (n - 1),)),
            dma((TOP_PIECES,)),
            dma((TOP_PIECES,)),
            dma((half // TILE,)),
            dma((half // TILE,)),
            dma((1,)),
        ],
        compiler_params=pltpu.CompilerParams(
            collective_id=0, has_side_effects=True, vmem_limit_bytes=60 * 1024 * 1024
        ),
    )(matrix, pivots.reshape(1, -1))
    col_ids = jnp.arange(cols, dtype=jnp.int32)
    keep_panel = (lax.axis_index("pcol") == 0) & (col_ids < pivots.shape[0])
    return jnp.where(keep_panel[None, :], matrix, stepped)


def solution(mesh):
    body = functools.partial(local, mesh.shape["prow"], mesh.shape["pcol"])
    return jax.shard_map(
        body, mesh=mesh, in_specs=(P("prow", "pcol"), P()),
        out_specs=P("prow", "pcol"), check_vma=False,
    )
```

```python
import functools

import jax
import jax.numpy as jnp
from jax import lax
from jax.experimental import pallas as pl
from jax.experimental.pallas import tpu as pltpu
from jax.sharding import PartitionSpec as P

MESH = pl.DeviceIdType.MESH
TOP_PIECES = 4
EARLY = 2
TILE = 256


def mm(a, b):
    return jnp.dot(a, b, preferred_element_type=jnp.float32)


def split(x):
    high = x.astype(jnp.bfloat16)
    low = (x - high.astype(jnp.float32)).astype(jnp.bfloat16)
    return high, low


def mm3(a, b):
    ah, al = split(a)
    bh, bl = split(b)
    return mm(ah, bh) + (mm(ah, bl) + mm(al, bh))


def kernel(
    procs, cols_procs, grid_x, a_ref, piv_ref, out_ref,
    abuf, top, hi, lo, cbuf, rbuf, gbuf, base, obuf, pan, l11, kbuf, proj,
    in_sem, ex_sem, pz_send, pz_recv, pp_sem, l_send, l_recv, k_sem,
    rs_send, rs_recv, ag_send, ag_recv,
    t_send, t_recv, p_send, p_recv, o_sem,
):
    B, cols = a_ref.shape
    half = cols // 2
    chips = procs // 2
    rc = B // chips
    rp = B // TOP_PIECES
    me = lax.axis_index("prow")
    z = lax.axis_index("pcol")
    chip = me // 2
    core = me % 2
    peer = chip * 2 + 1 - core

    def remote(src, dst, send, recv, device):
        return pltpu.make_async_remote_copy(
            src_ref=src, dst_ref=dst, send_sem=send, recv_sem=recv,
            device_id=device, device_id_type=MESH,
        )

    def snake(k):
        across, down = k % grid_x, k // grid_x
        return down * grid_x + across + down % 2 * (grid_x - 1 - 2 * across)

    def other(d):
        return (chip + d) % chips

    def rows_of(k):
        return pl.ds(pl.multiple_of(k * rc, rc), rc)

    mine = pl.ds(pl.multiple_of(core * half, half), half)
    theirs = pl.ds(pl.multiple_of((1 - core) * half, half), half)
    load = pltpu.make_async_copy(a_ref.at[:, mine], abuf.at[core], in_sem.at[0])
    load.start()
    load_panel = pltpu.make_async_copy(
        a_ref.at[:, pl.ds(0, B)], pan.at[core], in_sem.at[1]
    )

    @pl.when(z == 0)
    def _():
        load_panel.start()

    step = 1 - 2 * core
    place = snake(chip)
    rank = (place * step + chips) % chips
    onward = snake((place + step + chips) % chips) * 2 + core

    barrier = pltpu.get_barrier_semaphore()
    greeted = [(peer, z)]
    greeted += [(other(d) * 2 + core, z) for d in range(1, chips)]
    greeted += [(me, (z + d) % cols_procs) for d in range(1, cols_procs)]
    for device in greeted:
        pl.semaphore_signal(barrier, inc=1, device_id=device, device_id_type=MESH)

    row = lax.broadcasted_iota(jnp.int32, (B, B), 0)
    col = lax.broadcasted_iota(jnp.int32, (B, B), 1)
    eye = row == col
    piv = piv_ref[...]
    pr = jnp.broadcast_to(piv, (B, B))
    pc = jnp.sum(jnp.where(eye, pr, 0), axis=1, keepdims=True)
    colf = col.astype(jnp.float32)
    before = col < row

    def last(mask, lanes):
        return jnp.max(jnp.where(mask, lanes, -1.0), axis=1, keepdims=True)

    prev = last((pc == pr) & before, colf)
    parent = last((pr == row) & before, colf)
    root_self = parent < 0
    hot = jnp.where(
        root_self, jnp.where(eye, 1.0, 0.0), jnp.where(colf == parent, 1.0, 0.0)
    ).astype(jnp.bfloat16)
    pl.semaphore_wait(barrier, len(greeted))

    exchange = remote(
        a_ref.at[:, theirs], abuf.at[core], ex_sem.at[0], ex_sem.at[1], (peer, z)
    )
    exchange.start()

    panel_z = [
        remote(
            a_ref.at[:, pl.ds(0, B)], pan.at[core],
            pz_send.at[d - 1], pz_recv.at[0], (me, (z + d) % cols_procs),
        )
        for d in range(1, cols_procs)
    ]

    @pl.when(z == 0)
    def _():
        for copy in panel_z:
            copy.start()

    top_copies = [
        remote(
            top.at[pl.ds(i * rp, rp)], top.at[pl.ds(i * rp, rp)],
            t_send.at[i], t_recv.at[i], (onward, z),
        )
        for i in range(TOP_PIECES)
    ]

    load.wait()

    @pl.when(me == 0)
    def _():
        top[...] = abuf[0]
        for copy in top_copies[:EARLY]:
            copy.start()

    steps = 1
    while steps < B:
        hot = mm(hot, hot).astype(jnp.bfloat16)
        steps *= 2
    from_prev = mm(jnp.where(colf == prev, 1.0, 0.0).astype(jnp.bfloat16), hot)

    first = chip * (2 * B)
    col2 = lax.broadcasted_iota(jnp.int32, (B, 2 * B), 1)
    on_first = (chip == 0).astype(jnp.float32)
    direct = jnp.where((prev < 0) & (pc == col2 + first), 1.0, 0.0)
    pick = jnp.concatenate(
        [direct[:, :B] + on_first * from_prev, direct[:, B:]], axis=1
    ).astype(jnp.bfloat16)

    row2 = lax.broadcasted_iota(jnp.int32, (2 * B, B), 0)
    col3 = lax.broadcasted_iota(jnp.int32, (2 * B, B), 1).astype(jnp.float32)
    logical = row2 + first
    filled = last(jnp.broadcast_to(piv, (2 * B, B)) == logical, col3)
    is_rest = logical[:, :1] >= B
    fill = jnp.where((col3 == filled) & (logical >= B), 1.0, 0.0)
    fill = mm(fill.astype(jnp.bfloat16), hot).astype(jnp.bfloat16)
    keep = jnp.where(is_rest & (filled < 0), 1.0, 0.0)

    own_rows = pl.ds(pl.multiple_of(core * B, B), B)
    peer_rows = pl.ds(pl.multiple_of((1 - core) * B, B), B)
    h, l = split(abuf[core])
    hi[own_rows, :] = h
    lo[own_rows, :] = l

    exchange.wait_recv()

    @pl.when(me == 1)
    def _():
        top[...] = abuf[0]
        for copy in top_copies[:EARLY]:
            copy.start()

    h, l = split(abuf[1 - core])
    hi[peer_rows, :] = h
    lo[peer_rows, :] = l

    to_zero = remote(pan.at[core], pan.at[core], pp_sem.at[0], pp_sem.at[1], (peer, z))
    l_copies = [
        remote(pan.at[0], l11, l_send.at[d - 1], l_recv.at[0], (other(d) * 2 + core, z))
        for d in range(1, chips)
    ]

    for t in range(0, half, TILE):
        s = pl.ds(t, TILE)
        cbuf[:, s] = mm(pick, hi[:, s]) + mm(pick, lo[:, s])
    rs = [
        remote(
            cbuf.at[rows_of(other(d))], rbuf.at[d - 1],
            rs_send.at[d - 1], rs_recv.at[d - 1], (other(d) * 2 + core, z),
        )
        for d in range(1, chips)
    ]
    for copy in rs:
        copy.start()

    @pl.when(rank == 0)
    def _():
        for copy in top_copies[EARLY:]:
            copy.start()

    @pl.when(z != 0)
    def _():
        panel_z[0].wait_recv()

    @pl.when(z == 0)
    def _():
        load_panel.wait()

    @pl.when(core == 1)
    def _():
        to_zero.start()

    @pl.when(me == 0)
    def _():
        for copy in l_copies:
            copy.start()
        l11[...] = pan[0]

    def forward(i):
        @pl.when((rank > 0) & (rank < chips - 1))
        def _():
            top_copies[i].wait_recv()
            top_copies[i].start()

    proj[:, :] = fill

    forward(0)

    levels = []
    size = 2
    while size < B:
        levels.append(size)
        size *= 2

    def off_diagonal(size):
        same = (row & (-2 * size)) == (col & (-2 * size))
        return jnp.where(
            same & ((row & size) != 0) & ((col & size) == 0), l11[...], 0.0
        )

    def advance(sizes):
        @pl.when(core == 0)
        def _():
            x = kbuf[:B, :]
            for size in sizes:
                x = x - mm3(x, mm3(off_diagonal(size), x))
            kbuf[:B, :] = x

    forward(1)
    for copy in rs:
        copy.wait_recv()
    total = cbuf[rows_of(chip), :]
    for d in range(1, chips):
        total = total + rbuf[d - 1]
    gbuf[rows_of(chip), :] = total
    ag = [
        remote(
            gbuf.at[rows_of(chip)], gbuf.at[rows_of(chip)],
            ag_send.at[d - 1], ag_recv.at[d - 1], (other(d) * 2 + core, z),
        )
        for d in range(1, chips)
    ]
    for copy in ag:
        copy.start()
    forward(2)
    forward(3)
    @pl.when((core == 0) & (chip != 0))
    def _():
        l_copies[0].wait_recv()

    @pl.when(core == 0)
    def _():
        to_zero.wait_recv()

    @pl.when(core == 0)
    def _():
        kbuf[:B, :] = jnp.where(eye, 1.0, 0.0) - off_diagonal(1)

    cut = 0
    advance(levels[cut:])

    k_copy = remote(kbuf, kbuf, k_sem.at[0], k_sem.at[1], (peer, z))

    @pl.when(core == 0)
    def _():
        inverse = kbuf[:B, :]
        lead = on_first * jnp.where(eye, 1.0, 0.0) - (1.0 - on_first) * pan[0]
        low_part = mm3(pan[1], inverse)
        kbuf[:B, :] = mm3(lead, inverse)
        kbuf[B:, :] = -low_part
        k_copy.start()

    @pl.when(rank == chips - 1)
    def _():
        for copy in top_copies:
            copy.wait_recv()

    base[:B, :] = keep[:B] * abuf[0]
    base[B:, :] = keep[B:] * abuf[1]
    for t in range(0, half, TILE):
        s = pl.ds(t, TILE)
        th, tl = split(top[:, s])
        base[:, s] = base[:, s] + (mm(proj[...], th) + mm(proj[...], tl))

    @pl.when(core == 1)
    def _():
        k_copy.wait_recv()

    kh_peer, kl_peer = split(kbuf[peer_rows, :])
    kh_own, kl_own = split(kbuf[own_rows, :])
    for d in range(1, chips):
        came = rows_of((chip - d + chips) % chips)
        remote(
            gbuf.at[came], gbuf.at[came],
            ag_send.at[d - 1], ag_recv.at[d - 1], (other(d) * 2 + core, z),
        ).wait_recv()

    def tile_of(side, t):
        return pl.ds(pl.multiple_of(side * half + t, TILE), TILE)

    tiles = range(0, half, TILE)
    out_peer = [
        remote(
            obuf.at[0, :, pl.ds(t, TILE)], out_ref.at[:, tile_of(core, t)],
            p_send.at[t // TILE], p_recv.at[t // TILE], (peer, z),
        )
        for t in tiles
    ]
    out_own = pltpu.make_async_copy(obuf.at[1], out_ref.at[:, mine], o_sem.at[0])
    def keep_panel(slot, side, t):
        if t == 0:
            @pl.when((z == 0) & (core == 0))
            def _():
                obuf[slot, :, :B] = abuf[side, :, :B]

    for t in tiles:
        s = pl.ds(t, TILE)
        gh, gl = split(gbuf[:, s])
        obuf[0, :, s] = base[peer_rows, s] + (
            mm(kh_peer, gh) + (mm(kh_peer, gl) + mm(kl_peer, gh))
        )
        keep_panel(0, 1 - core, t)
        out_peer[t // TILE].start()
    for t in tiles:
        s = pl.ds(t, TILE)
        gh, gl = split(gbuf[:, s])
        obuf[1, :, s] = base[own_rows, s] + (
            mm(kh_own, gh) + (mm(kh_own, gl) + mm(kl_own, gh))
        )
    keep_panel(1, core, 0)
    out_own.start()

    exchange.wait_send()

    @pl.when(z == 0)
    def _():
        for copy in panel_z:
            copy.wait_send()

    @pl.when(core == 1)
    def _():
        to_zero.wait_send()

    @pl.when(core == 0)
    def _():
        k_copy.wait_send()

    @pl.when(me == 0)
    def _():
        for copy in l_copies:
            copy.wait_send()

    @pl.when(rank < chips - 1)
    def _():
        for copy in top_copies:
            copy.wait_send()

    for copy in rs + ag:
        copy.wait_send()
    out_own.wait()
    for t in tiles:
        remote(
            obuf.at[0, :, pl.ds(t, TILE)], out_ref.at[:, tile_of(1 - core, t)],
            p_send.at[t // TILE], p_recv.at[t // TILE], (peer, z),
        ).wait_recv()
    for copy in out_peer:
        copy.wait_send()


def local(procs, cols_procs, matrix, pivots):
    B, cols = matrix.shape
    half = cols // 2
    chips = procs // 2
    n = 1
    while n * n < chips:
        n += 1
    f32, bf16 = jnp.float32, jnp.bfloat16
    dma = pltpu.SemaphoreType.DMA
    stepped = pl.pallas_call(
        functools.partial(kernel, procs, cols_procs, n),
        out_shape=jax.ShapeDtypeStruct((B, cols), f32),
        in_specs=[
            pl.BlockSpec(memory_space=pltpu.HBM),
            pl.BlockSpec(memory_space=pltpu.VMEM),
        ],
        out_specs=pl.BlockSpec(memory_space=pl.ANY),
        scratch_shapes=[
            pltpu.VMEM((2, B, half), f32),
            pltpu.VMEM((B, half), f32),
            pltpu.VMEM((2 * B, half), bf16),
            pltpu.VMEM((2 * B, half), bf16),
            pltpu.VMEM((B, half), f32),
            pltpu.VMEM((chips - 1, B // chips, half), f32),
            pltpu.VMEM((B, half), f32),
            pltpu.VMEM((2 * B, half), f32),
            pltpu.VMEM((2, B, half), f32),
            pltpu.VMEM((2, B, B), f32),
            pltpu.VMEM((B, B), f32),
            pltpu.VMEM((2 * B, B), f32),
            pltpu.VMEM((2 * B, B), bf16),
            dma((2,)),
            dma((2,)),
            dma((cols_procs - 1,)),
            dma((1,)),
            dma((2,)),
            dma((chips - 1,)),
            dma((1,)),
            dma((2,)),
            dma((chips - 1,)),
            dma((chips - 1,)),
            dma((chips - 1,)),
            dma((chips - 1,)),
            dma((TOP_PIECES,)),
            dma((TOP_PIECES,)),
            dma((half // TILE,)),
            dma((half // TILE,)),
            dma((1,)),
        ],
        compiler_params=pltpu.CompilerParams(
            collective_id=0, has_side_effects=True, vmem_limit_bytes=16 * 1024 * 1024
        ),
    )(matrix, pivots.reshape(1, -1))
    return stepped


def solution(mesh):
    body = functools.partial(local, mesh.shape["prow"], mesh.shape["pcol"])
    return jax.shard_map(
        body, mesh=mesh, in_specs=(P("prow", "pcol"), P()),
        out_specs=P("prow", "pcol"), check_vma=False,
    )
```

```python
import functools

import jax
import jax.numpy as jnp
from jax import lax
from jax.experimental import pallas as pl
from jax.experimental.pallas import tpu as pltpu
from jax.sharding import PartitionSpec as P

MESH = pl.DeviceIdType.MESH
TOP_PIECES = 4
EARLY = 1
TILE = 256


def mm(a, b):
    return jnp.dot(a, b, preferred_element_type=jnp.float32)


def split(x):
    high = x.astype(jnp.bfloat16)
    low = (x - high.astype(jnp.float32)).astype(jnp.bfloat16)
    return high, low


def mm3(a, b):
    ah, al = split(a)
    bh, bl = split(b)
    return mm(ah, bh) + (mm(ah, bl) + mm(al, bh))


def kernel(
    procs, cols_procs, grid_x, a_ref, piv_ref, out_ref,
    abuf, top, hi, lo, cbuf, rbuf, gbuf, base, obuf, pan, l11, kbuf, proj,
    in_sem, ex_sem, pz_send, pz_recv, pp_sem, l_send, l_recv, k_sem,
    rs_send, rs_recv, ag_send, ag_recv,
    t_send, t_recv, p_send, p_recv, o_sem,
):
    B, cols = a_ref.shape
    half = cols // 2
    chips = procs // 2
    rc = B // chips
    rp = B // TOP_PIECES
    me = lax.axis_index("prow")
    z = lax.axis_index("pcol")
    chip = me // 2
    core = me % 2
    peer = chip * 2 + 1 - core

    def remote(src, dst, send, recv, device):
        return pltpu.make_async_remote_copy(
            src_ref=src, dst_ref=dst, send_sem=send, recv_sem=recv,
            device_id=device, device_id_type=MESH,
        )

    def snake(k):
        across, down = k % grid_x, k // grid_x
        return down * grid_x + across + down % 2 * (grid_x - 1 - 2 * across)

    def other(d):
        return (chip + d) % chips

    def rows_of(k):
        return pl.ds(pl.multiple_of(k * rc, rc), rc)

    mine = pl.ds(pl.multiple_of(core * half, half), half)
    theirs = pl.ds(pl.multiple_of((1 - core) * half, half), half)
    load = pltpu.make_async_copy(a_ref.at[:, mine], abuf.at[core], in_sem.at[0])
    load.start()
    load_panel = pltpu.make_async_copy(
        a_ref.at[:, pl.ds(0, B)], pan.at[core], in_sem.at[1]
    )

    @pl.when(z == 0)
    def _():
        load_panel.start()

    step = 1 - 2 * core
    place = snake(chip)
    rank = (place * step + chips) % chips
    onward = snake((place + step + chips) % chips) * 2 + core

    barrier = pltpu.get_barrier_semaphore()
    greeted = [(peer, z)]
    greeted += [(other(d) * 2 + core, z) for d in range(1, chips)]
    greeted += [(me, (z + d) % cols_procs) for d in range(1, cols_procs)]
    for device in greeted:
        pl.semaphore_signal(barrier, inc=1, device_id=device, device_id_type=MESH)

    row = lax.broadcasted_iota(jnp.int32, (B, B), 0)
    col = lax.broadcasted_iota(jnp.int32, (B, B), 1)
    eye = row == col
    piv = piv_ref[...]
    pr = jnp.broadcast_to(piv, (B, B))
    pc = jnp.sum(jnp.where(eye, pr, 0), axis=1, keepdims=True)
    colf = col.astype(jnp.float32)
    before = col < row

    def last(mask, lanes):
        return jnp.max(jnp.where(mask, lanes, -1.0), axis=1, keepdims=True)

    prev = last((pc == pr) & before, colf)
    parent = last((pr == row) & before, colf)
    root_self = parent < 0
    hot = jnp.where(
        root_self, jnp.where(eye, 1.0, 0.0), jnp.where(colf == parent, 1.0, 0.0)
    ).astype(jnp.bfloat16)
    pl.semaphore_wait(barrier, len(greeted))

    exchange = remote(
        a_ref.at[:, theirs], abuf.at[core], ex_sem.at[0], ex_sem.at[1], (peer, z)
    )
    exchange.start()

    panel_z = [
        remote(
            a_ref.at[:, pl.ds(0, B)], pan.at[core],
            pz_send.at[d - 1], pz_recv.at[0], (me, (z + d) % cols_procs),
        )
        for d in range(1, cols_procs)
    ]

    @pl.when(z == 0)
    def _():
        for copy in panel_z:
            copy.start()

    top_copies = [
        remote(
            top.at[pl.ds(i * rp, rp)], top.at[pl.ds(i * rp, rp)],
            t_send.at[i], t_recv.at[i], (onward, z),
        )
        for i in range(TOP_PIECES)
    ]

    load.wait()

    @pl.when(me == 0)
    def _():
        top[...] = abuf[0]
        for copy in top_copies[:EARLY]:
            copy.start()

    steps = 1
    while steps < B:
        hot = mm(hot, hot).astype(jnp.bfloat16)
        steps *= 2
    from_prev = mm(jnp.where(colf == prev, 1.0, 0.0).astype(jnp.bfloat16), hot)

    first = chip * (2 * B)
    col2 = lax.broadcasted_iota(jnp.int32, (B, 2 * B), 1)
    on_first = (chip == 0).astype(jnp.float32)
    direct = jnp.where((prev < 0) & (pc == col2 + first), 1.0, 0.0)
    pick = jnp.concatenate(
        [direct[:, :B] + on_first * from_prev, direct[:, B:]], axis=1
    ).astype(jnp.bfloat16)

    row2 = lax.broadcasted_iota(jnp.int32, (2 * B, B), 0)
    col3 = lax.broadcasted_iota(jnp.int32, (2 * B, B), 1).astype(jnp.float32)
    logical = row2 + first
    filled = last(jnp.broadcast_to(piv, (2 * B, B)) == logical, col3)
    is_rest = logical[:, :1] >= B
    fill = jnp.where((col3 == filled) & (logical >= B), 1.0, 0.0)
    fill = mm(fill.astype(jnp.bfloat16), hot).astype(jnp.bfloat16)
    keep = jnp.where(is_rest & (filled < 0), 1.0, 0.0)

    own_rows = pl.ds(pl.multiple_of(core * B, B), B)
    peer_rows = pl.ds(pl.multiple_of((1 - core) * B, B), B)
    h, l = split(abuf[core])
    hi[own_rows, :] = h
    lo[own_rows, :] = l

    exchange.wait_recv()

    @pl.when(me == 1)
    def _():
        top[...] = abuf[0]
        for copy in top_copies[:EARLY]:
            copy.start()

    h, l = split(abuf[1 - core])
    hi[peer_rows, :] = h
    lo[peer_rows, :] = l

    to_zero = remote(pan.at[core], pan.at[core], pp_sem.at[0], pp_sem.at[1], (peer, z))
    l_copies = [
        remote(pan.at[0], l11, l_send.at[d - 1], l_recv.at[0], (other(d) * 2 + core, z))
        for d in range(1, chips)
    ]

    for t in range(0, half, TILE):
        s = pl.ds(t, TILE)
        cbuf[:, s] = mm(pick, hi[:, s]) + mm(pick, lo[:, s])
    rs = [
        remote(
            cbuf.at[rows_of(other(d))], rbuf.at[d - 1],
            rs_send.at[d - 1], rs_recv.at[d - 1], (other(d) * 2 + core, z),
        )
        for d in range(1, chips)
    ]
    for copy in rs:
        copy.start()

    @pl.when(rank == 0)
    def _():
        for copy in top_copies[EARLY:]:
            copy.start()

    @pl.when(z != 0)
    def _():
        panel_z[0].wait_recv()

    @pl.when(z == 0)
    def _():
        load_panel.wait()

    @pl.when(core == 1)
    def _():
        to_zero.start()

    @pl.when(me == 0)
    def _():
        for copy in l_copies:
            copy.start()
        l11[...] = pan[0]

    def forward(i):
        @pl.when((rank > 0) & (rank < chips - 1))
        def _():
            top_copies[i].wait_recv()
            top_copies[i].start()

    proj[:, :] = fill

    forward(0)

    levels = []
    size = 2
    while size < B:
        levels.append(size)
        size *= 2

    def off_diagonal(size):
        same = (row & (-2 * size)) == (col & (-2 * size))
        return jnp.where(
            same & ((row & size) != 0) & ((col & size) == 0), l11[...], 0.0
        )

    def advance(sizes):
        @pl.when(core == 0)
        def _():
            x = kbuf[:B, :]
            for size in sizes:
                x = x - mm3(x, mm3(off_diagonal(size), x))
            kbuf[:B, :] = x

    forward(1)
    for copy in rs:
        copy.wait_recv()
    total = cbuf[rows_of(chip), :]
    for d in range(1, chips):
        total = total + rbuf[d - 1]
    gbuf[rows_of(chip), :] = total
    ag = [
        remote(
            gbuf.at[rows_of(chip)], gbuf.at[rows_of(chip)],
            ag_send.at[d - 1], ag_recv.at[d - 1], (other(d) * 2 + core, z),
        )
        for d in range(1, chips)
    ]
    for copy in ag:
        copy.start()
    forward(2)
    forward(3)
    @pl.when((core == 0) & (chip != 0))
    def _():
        l_copies[0].wait_recv()

    @pl.when(core == 0)
    def _():
        to_zero.wait_recv()

    @pl.when(core == 0)
    def _():
        kbuf[:B, :] = jnp.where(eye, 1.0, 0.0) - off_diagonal(1)

    cut = 0
    advance(levels[cut:])

    k_copy = remote(kbuf, kbuf, k_sem.at[0], k_sem.at[1], (peer, z))

    @pl.when(core == 0)
    def _():
        inverse = kbuf[:B, :]
        lead = on_first * jnp.where(eye, 1.0, 0.0) - (1.0 - on_first) * pan[0]
        low_part = mm3(pan[1], inverse)
        kbuf[:B, :] = mm3(lead, inverse)
        kbuf[B:, :] = -low_part
        k_copy.start()

    @pl.when(rank == chips - 1)
    def _():
        for copy in top_copies:
            copy.wait_recv()

    base[:B, :] = keep[:B] * abuf[0]
    base[B:, :] = keep[B:] * abuf[1]
    for t in range(0, half, TILE):
        s = pl.ds(t, TILE)
        th, tl = split(top[:, s])
        base[:, s] = base[:, s] + (mm(proj[...], th) + mm(proj[...], tl))

    @pl.when(core == 1)
    def _():
        k_copy.wait_recv()

    kh_peer, kl_peer = split(kbuf[peer_rows, :])
    kh_own, kl_own = split(kbuf[own_rows, :])
    for d in range(1, chips):
        came = rows_of((chip - d + chips) % chips)
        remote(
            gbuf.at[came], gbuf.at[came],
            ag_send.at[d - 1], ag_recv.at[d - 1], (other(d) * 2 + core, z),
        ).wait_recv()

    def tile_of(side, t):
        return pl.ds(pl.multiple_of(side * half + t, TILE), TILE)

    tiles = range(0, half, TILE)
    out_peer = [
        remote(
            obuf.at[0, :, pl.ds(t, TILE)], out_ref.at[:, tile_of(core, t)],
            p_send.at[t // TILE], p_recv.at[t // TILE], (peer, z),
        )
        for t in tiles
    ]
    out_own = pltpu.make_async_copy(obuf.at[1], out_ref.at[:, mine], o_sem.at[0])
    def keep_panel(slot, side, t):
        if t == 0:
            @pl.when((z == 0) & (core == 0))
            def _():
                obuf[slot, :, :B] = abuf[side, :, :B]

    for t in tiles:
        s = pl.ds(t, TILE)
        gh, gl = split(gbuf[:, s])
        obuf[0, :, s] = base[peer_rows, s] + (
            mm(kh_peer, gh) + (mm(kh_peer, gl) + mm(kl_peer, gh))
        )
        keep_panel(0, 1 - core, t)
        out_peer[t // TILE].start()
    for t in tiles:
        s = pl.ds(t, TILE)
        gh, gl = split(gbuf[:, s])
        obuf[1, :, s] = base[own_rows, s] + (
            mm(kh_own, gh) + (mm(kh_own, gl) + mm(kl_own, gh))
        )
    keep_panel(1, core, 0)
    out_own.start()

    exchange.wait_send()

    @pl.when(z == 0)
    def _():
        for copy in panel_z:
            copy.wait_send()

    @pl.when(core == 1)
    def _():
        to_zero.wait_send()

    @pl.when(core == 0)
    def _():
        k_copy.wait_send()

    @pl.when(me == 0)
    def _():
        for copy in l_copies:
            copy.wait_send()

    @pl.when(rank < chips - 1)
    def _():
        for copy in top_copies:
            copy.wait_send()

    for copy in rs + ag:
        copy.wait_send()
    out_own.wait()
    for t in tiles:
        remote(
            obuf.at[0, :, pl.ds(t, TILE)], out_ref.at[:, tile_of(1 - core, t)],
            p_send.at[t // TILE], p_recv.at[t // TILE], (peer, z),
        ).wait_recv()
    for copy in out_peer:
        copy.wait_send()


def local(procs, cols_procs, matrix, pivots):
    B, cols = matrix.shape
    half = cols // 2
    chips = procs // 2
    n = 1
    while n * n < chips:
        n += 1
    f32, bf16 = jnp.float32, jnp.bfloat16
    dma = pltpu.SemaphoreType.DMA
    stepped = pl.pallas_call(
        functools.partial(kernel, procs, cols_procs, n),
        out_shape=jax.ShapeDtypeStruct((B, cols), f32),
        in_specs=[
            pl.BlockSpec(memory_space=pltpu.HBM),
            pl.BlockSpec(memory_space=pltpu.VMEM),
        ],
        out_specs=pl.BlockSpec(memory_space=pl.ANY),
        scratch_shapes=[
            pltpu.VMEM((2, B, half), f32),
            pltpu.VMEM((B, half), f32),
            pltpu.VMEM((2 * B, half), bf16),
            pltpu.VMEM((2 * B, half), bf16),
            pltpu.VMEM((B, half), f32),
            pltpu.VMEM((chips - 1, B // chips, half), f32),
            pltpu.VMEM((B, half), f32),
            pltpu.VMEM((2 * B, half), f32),
            pltpu.VMEM((2, B, half), f32),
            pltpu.VMEM((2, B, B), f32),
            pltpu.VMEM((B, B), f32),
            pltpu.VMEM((2 * B, B), f32),
            pltpu.VMEM((2 * B, B), bf16),
            dma((2,)),
            dma((2,)),
            dma((cols_procs - 1,)),
            dma((1,)),
            dma((2,)),
            dma((chips - 1,)),
            dma((1,)),
            dma((2,)),
            dma((chips - 1,)),
            dma((chips - 1,)),
            dma((chips - 1,)),
            dma((chips - 1,)),
            dma((TOP_PIECES,)),
            dma((TOP_PIECES,)),
            dma((half // TILE,)),
            dma((half // TILE,)),
            dma((1,)),
        ],
        compiler_params=pltpu.CompilerParams(
            collective_id=0, has_side_effects=True, vmem_limit_bytes=16 * 1024 * 1024
        ),
    )(matrix, pivots.reshape(1, -1))
    return stepped


def solution(mesh):
    body = functools.partial(local, mesh.shape["prow"], mesh.shape["pcol"])
    return jax.shard_map(
        body, mesh=mesh, in_specs=(P("prow", "pcol"), P()),
        out_specs=P("prow", "pcol"), check_vma=False,
    )
```
